32 devices in a mesh: dp: 32 (over z, y, x, core).
Axes of the slice: x: 2, y: 2, z: 4, core: 2. Of those that a mesh axis runs over, the one named last changes fastest.
Arguments:
- hidden_in: bfloat16 [64, 128, 1024], P('dp'), may hold values from -6 to 6
- segments: int32 [64, 128], P('dp'), may hold values from 0 to 3, never falling along the last dimension, each value on 1 to 64 neighbouring positions
- cotangent: bfloat16 [64, 128, 1024], P('dp'), may hold values from -6 to 6
- pre_gain: bfloat16 [1024], P('dp'), may hold values from 0.099609375 to 1.8984375
- proj_weight: bfloat16 [1024, 4352], P('dp'), may hold values from -0.1875 to 0.1875
- step_weight: bfloat16 [1024, 32], P('dp'), may hold values from -0.1875 to 0.1875
- conv_weight: bfloat16 [2304, 4], P('dp'), may hold values from -3 to 3
- conv_bias: bfloat16 [2304], P('dp'), may hold values from -3 to 3
- gate_gain: bfloat16 [2048], P('dp'), may hold values from 0.099609375 to 1.8984375
- out_weight: bfloat16 [2048, 1024], P('dp'), may hold values from -0.125 to 0.125
- decay_log: float32 [32], replicated, may hold values from -5 to -1
- step_bias: float32 [32], replicated, may hold values from -3 to 0
- skip_gain: float32 [32], replicated, may hold values from 0.5 to 2
Outputs:
- output: bfloat16 [64, 128, 1024], P('dp')
- input_grad: float32 [64, 128, 1024], P('dp')
- grad_pre_gain: float32 [1024], P('dp')
- grad_proj_weight: float32 [1024, 4352], P('dp')
- grad_step_weight: float32 [1024, 32], P('dp')
- grad_conv_weight: float32 [2304, 4], P('dp')
- grad_conv_bias: float32 [2304], P('dp')
- grad_gate_gain: float32 [2048], P('dp')
- grad_out_weight: float32 [2048, 1024], P('dp')
- grad_decay_log: float32 [32], replicated
- grad_step_bias: float32 [32], replicated
- grad_skip_gain: float32 [32], replicated
The draws below stay inside these ranges and needn't reach their ends.
Inputs may be any that keep to these rules, and one draw needn't show every extreme that they name: `segments`: in each row of 128 positions the numbers never fall, and each number covers at most 64 positions.
All inputs are finite; a program needn't handle non-finite values.
Results may differ from the reference program's by a relative error of at most 0.0071.
Values may be sent and summed in bfloat16 or wider, within the bound.
A program may use at most 192 MiB of HBM per device.

```python
import math
import jax
import jax.numpy as jnp
import numpy as np
from jax import lax

D = 1024
HEADS = 32
KERNEL = 4
SPAN = 256
SEQ = 128
INNER = 2048
PROJ = 4352
CONV = 2304
ROWS = 64


def spiked(drawn, own_key, source, target, parts, factor):
    def block_of(position):
        return (jnp.arange(drawn.shape[position]) // (drawn.shape[position] // parts)).reshape((-1,) + (1,) * (drawn.ndim - 1 - position))

    first = jax.random.permutation(own_key, parts)[block_of(target)]
    far = (block_of(target) + parts // 2) % parts
    return jnp.where((block_of(source) == first) | (block_of(source) == far), factor * drawn, drawn)


def steps_of(stream_key, dims, shards, smallest, largest):
    gain = 1.0
    for axis_at, blocks in shards:
        heights = jax.random.uniform(jax.random.fold_in(jax.random.fold_in(stream_key, 6), axis_at), (blocks,), jnp.float32, smallest / len(shards), largest / len(shards))
        gain = gain * jnp.repeat(jnp.exp(heights), dims[axis_at] // blocks).reshape((-1,) + (1,) * (len(dims) - 1 - axis_at))
    return gain


def length_profile(amount, total, bound, slope):
    loads = [(1 << 20) // math.isqrt(rank ** slope) + 1 for rank in range(2, amount + 1)]
    rest, counts = total - bound - (amount - 1), [1] * (amount - 1)
    while rest > 0:
        movable = [i for i in range(amount - 1) if counts[i] < bound]
        whole, remaining = sum([loads[i] for i in movable]), rest
        for i in movable:
            more = min(bound - counts[i], max(1, remaining * loads[i] // whole), rest)
            counts[i] = counts[i] + more
            rest = rest - more
    return np.array([bound] + counts)


def ragged(stream_key, amount, total, limit, slope):
    if amount == 2:
        one = jax.random.randint(stream_key, (), max(1, total - limit), min(limit, total - 1) + 1)
        return jnp.stack([one, total - one])
    lengths = jnp.asarray(length_profile(amount, total, limit, slope), jnp.int32)
    twos = (amount - 1) // 2
    donor, taker = lengths[1:1 + 2 * twos:2], lengths[2:2 + 2 * twos:2]
    room = jnp.minimum(donor - 1, limit - taker)
    moved = jax.random.randint(jax.random.fold_in(stream_key, 1), (twos,), 0, 1 << 20) % (room + 1)
    lengths = lengths.at[1:1 + 2 * twos:2].set(donor - moved).at[2:2 + 2 * twos:2].set(taker + moved)
    return lengths[jax.random.permutation(jax.random.fold_in(stream_key, 2), amount)]


def centred(stream_key, shape, scale, limit, cuts=(), kind=jnp.bfloat16):
    entries = jax.random.normal(stream_key, shape, jnp.float32) * scale
    if len(cuts) > 0:
        entries = steps_of(stream_key, shape, cuts, -0.22, 0.18) * entries
    return jnp.clip(entries, min=-limit, max=limit).astype(kind)


def gaussian_with(stream_key, extent, width, limit, shards, heavy, held_as=jnp.bfloat16):
    values = width * jax.random.normal(stream_key, extent, jnp.float32)
    if shards:
        values = values * steps_of(stream_key, extent, shards, -0.22, 0.18)
    return jnp.clip(spiked(values, jax.random.fold_in(stream_key, 3), *heavy), -limit, limit).astype(held_as)


def setup_inputs(seed: int = 0) -> dict:
    streams_of = jax.random.split(jax.random.key(seed), 14)
    hidden_in = gaussian_with(streams_of[0], (ROWS, SEQ, D), 1.0, 6.0, ((0, 32),), (0, 2, 32, 2.75))
    segments = jax.vmap(lambda own: jnp.searchsorted(jnp.cumsum(ragged(own, 4, SEQ, SEQ // 2, 0)), jnp.arange(SEQ), side="right"))(jax.random.split(streams_of[1], ROWS)).reshape((ROWS, SEQ)).astype(jnp.int32)
    cotangent = centred(streams_of[2], (ROWS, SEQ, D), 1.0, 6.0, ((0, 32),))
    pre_gain = jnp.clip(1.0 + 0.18 * jax.random.normal(streams_of[3], (D,), jnp.float32), 0.099609375, 1.8984375).astype(jnp.bfloat16)
    proj_weight = centred(streams_of[4], (D, PROJ), D ** -0.5, 0.1875, ((0, 32),))
    step_weight = centred(streams_of[5], (D, HEADS), D ** -0.5, 0.1875, ((0, 32),))
    conv_weight = centred(streams_of[6], (CONV, KERNEL), KERNEL ** -0.5, 3.0, ((0, 32),))
    conv_bias = centred(streams_of[7], (CONV,), 0.5, 3.0, ((0, 32),))
    gate_gain = jnp.clip(1.0 + 0.18 * jax.random.normal(streams_of[8], (INNER,), jnp.float32), 0.099609375, 1.8984375).astype(jnp.bfloat16)
    out_weight = centred(streams_of[9], (INNER, D), INNER ** -0.5, 0.125, ((0, 32),))
    decay_log = jnp.clip(jax.random.uniform(streams_of[10], (HEADS,), jnp.float32, -5.0, -1.0), -5.0, -1.0)
    step_bias = jnp.clip(jax.random.uniform(streams_of[11], (HEADS,), jnp.float32, -3.0, 0.0), -3.0, 0.0)
    skip_gain = jnp.clip(jax.random.uniform(streams_of[12], (HEADS,), jnp.float32, 0.5, 2.0), 0.5, 2.0)
    return {"hidden_in": hidden_in, "segments": segments, "cotangent": cotangent, "pre_gain": pre_gain, "proj_weight": proj_weight, "step_weight": step_weight, "conv_weight": conv_weight, "conv_bias": conv_bias, "gate_gain": gate_gain, "out_weight": out_weight, "decay_log": decay_log, "step_bias": step_bias, "skip_gain": skip_gain}


exact = lax.Precision.HIGHEST

@jax.custom_vjp
def low(v):
    return lax.optimization_barrier(v.astype(jnp.bfloat16)).astype(jnp.float32)

@jax.custom_vjp
def low_back(v):
    return v

def low_keep(v):
    return (low(v), None)

def low_pass(kept, grad):
    return (grad,)

def back_keep(v):
    return (v, None)

def back_low(kept, grad):
    return (low(grad),)
low.defvjp(low_keep, low_pass)
low_back.defvjp(back_keep, back_low)

def prenorm(rows_value, gain_value):
    inverse_rms = lax.rsqrt(lax.optimization_barrier(jnp.mean(rows_value * rows_value, -1, keepdims=True)) + 1e-05)
    return rows_value * inverse_rms * gain_value

def ssd_mixer(proj_out, step_raw, conv_weight, conv_bias, step_bias, decay_log, skip_gain, gate_gain, segment):
    length = proj_out.shape[0]
    head_count = step_raw.shape[1]
    inner_size = gate_gain.shape[0]
    state_size = (proj_out.shape[1] - 2 * inner_size) // 2
    kernel = conv_weight.shape[1]
    gate_part = proj_out[:, :inner_size]
    stream = proj_out[:, inner_size:]
    convolved = conv_bias + stream * conv_weight[:, kernel - 1]
    for offset in range(1, kernel):
        shifted = jnp.concatenate([jnp.zeros((offset, stream.shape[1]), stream.dtype), stream[:-offset]], 0)
        earlier = jnp.concatenate([jnp.full((offset,), -1, jnp.int32), segment[:-offset]], 0)
        same_doc = (earlier == segment).astype(stream.dtype)[:, None]
        convolved = convolved + same_doc * shifted * conv_weight[:, kernel - 1 - offset]
    activated = jax.nn.silu(convolved)
    channels = inner_size // head_count
    values = activated[:, :inner_size].reshape(length, head_count, channels)
    input_map = activated[:, inner_size:inner_size + state_size]
    output_map = activated[:, inner_size + state_size:]
    step_size = jax.nn.softplus(step_raw + step_bias)
    log_decay = -jnp.exp(decay_log) * step_size
    scaled = values * step_size[:, :, None]
    block_len = min(SPAN, length)
    block_count = length // block_len
    seg_blocks = segment.reshape(block_count, block_len)
    previous = jnp.concatenate([jnp.full((1,), -1, jnp.int32), seg_blocks[:-1, -1]], 0)
    resumes = (seg_blocks == previous[:, None]).astype(stream.dtype)
    carry_on = (seg_blocks[:, -1] == previous).astype(stream.dtype)
    to_last = (seg_blocks == seg_blocks[:, -1:]).astype(stream.dtype)
    causal = jnp.arange(block_len)[:, None] >= jnp.arange(block_len)[None, :]
    inside = ((seg_blocks[:, :, None] == seg_blocks[:, None, :]) & causal[None]).astype(stream.dtype)

    def one_block(state_now, pieces):
        decay_b, scaled_b, in_b, out_b, resume_b, carry_b, inside_b, values_b, last_b = pieces
        cumulative = jnp.cumsum(decay_b, 0)
        log_gap = cumulative[:, None, :] - cumulative[None, :, :]
        within = inside_b[:, :, None]
        decay_mat = jnp.exp(jnp.where(within > 0.5, log_gap, 0.0)) * within
        scores = jnp.dot(out_b, in_b.T, precision=exact)
        within_sum = jnp.einsum('tuh,uhp->thp', decay_mat * scores[:, :, None], scaled_b, precision=exact)
        recalled = jnp.einsum('tn,hpn->thp', out_b, state_now, precision=exact)
        recalled = recalled * (jnp.exp(cumulative) * resume_b[:, None])[:, :, None]
        result = within_sum + recalled + skip_gain[None, :, None] * values_b
        to_end = jnp.exp(cumulative[-1][None, :] - cumulative) * last_b[:, None]
        incoming = jnp.einsum('uh,uhp,un->hpn', to_end, scaled_b, in_b, precision=exact)
        state_next = state_now * (jnp.exp(cumulative[-1]) * carry_b)[:, None, None] + incoming
        return (state_next, result)
    pieces = (log_decay.reshape(block_count, block_len, head_count), scaled.reshape(block_count, block_len, head_count, channels), input_map.reshape(block_count, block_len, state_size), output_map.reshape(block_count, block_len, state_size), resumes, carry_on, inside, values.reshape(block_count, block_len, head_count, channels), to_last)
    zero_state = jnp.zeros((head_count, channels, state_size), stream.dtype)
    _, blocks_out = lax.scan(jax.checkpoint(one_block), zero_state, pieces)
    mixed = blocks_out.reshape(length, inner_size)
    gated = mixed * jax.nn.silu(gate_part)
    inverse_rms = lax.rsqrt(lax.optimization_barrier(jnp.mean(gated * gated, -1, keepdims=True)) + 1e-05)
    return gated * inverse_rms * gate_gain

def block_forward(rows_value, segment, pre_gain, proj_weight, step_weight, conv_weight, conv_bias, gate_gain, out_weight, decay_log, step_bias, skip_gain):
    normed = low(prenorm(rows_value, pre_gain))
    proj_out = low_back(jnp.einsum('gld,dk->glk', normed, proj_weight, precision=exact))
    step_raw = low_back(jnp.einsum('gld,dk->glk', normed, step_weight, precision=exact))
    mixed = jax.vmap(ssd_mixer, in_axes=(0, 0, None, None, None, None, None, None, 0))(proj_out, step_raw, conv_weight, conv_bias, step_bias, decay_log, skip_gain, gate_gain, segment)
    gated = low(mixed)
    return rows_value + jnp.einsum('glk,kd->gld', gated, out_weight, precision=exact)

def reference(hidden_in, segments, cotangent, pre_gain, proj_weight, step_weight, conv_weight, conv_bias, gate_gain, out_weight, decay_log, step_bias, skip_gain):
    params = (pre_gain, proj_weight, step_weight, conv_weight, conv_bias, gate_gain, out_weight, decay_log, step_bias, skip_gain)
    params = tuple((tensor.astype(jnp.float32) for tensor in params))
    group_rows = math.gcd(ROWS, max(1, 4096 // SEQ))
    group_count = ROWS // group_rows
    rows_all = hidden_in.astype(jnp.float32).reshape(group_count, group_rows, SEQ, D)
    segs_all = segments.reshape(group_count, group_rows, SEQ)
    cot_all = cotangent.astype(jnp.float32).reshape(group_count, group_rows, SEQ, D)

    def group_step(totals, pieces):
        rows_in, segment, upstream = pieces

        def forward(rows_value, *weights):
            return block_forward(rows_value, segment, *weights)
        result, pullback = jax.vjp(forward, rows_in, *params)
        gradients = pullback(upstream)
        totals = tuple((running + fresh_grad for running, fresh_grad in zip(totals, gradients[1:])))
        return (totals, (result.astype(jnp.bfloat16), gradients[0]))
    zeros = tuple((jnp.zeros_like(tensor) for tensor in params))
    totals, (outputs, in_grads) = lax.scan(group_step, zeros, (rows_all, segs_all, cot_all))
    return (outputs.reshape(ROWS, SEQ, D), in_grads.reshape(ROWS, SEQ, D)) + tuple(totals)
```

```python
import jax
import jax.numpy as jnp
from jax import lax
from jax.sharding import PartitionSpec as P

f32 = jnp.float32
bf16 = jnp.bfloat16
near = lax.Precision.HIGH


def contract_last(left, right):
    return lax.dot_general(left, right, (((1,), (1,)), ((), ())), preferred_element_type=f32)


def contract_first(left, right):
    return lax.dot_general(left, right, (((0,), (0,)), ((), ())), preferred_element_type=f32)


def orders(bits):
    rest = list(range(1, bits))
    other = rest[:]
    if len(rest) > 1:
        other[0], other[1] = rest[1], rest[0]
    return [0] + rest, [0] + other


def swap(value, total, bit):
    return lax.ppermute(value, "dp", [(i, i ^ (1 << bit)) for i in range(total)])


def mine_of(me, bit):
    return lax.rem(lax.div(me, 1 << bit), 2)


def gather_rows(shard, total, me, order):
    held = shard[None]
    done = []
    for bit in reversed(order):
        got = swap(held, total, bit)
        side = mine_of(me, bit) == 0
        first, second = jnp.where(side, held, got), jnp.where(side, got, held)
        lower = 1
        for earlier in done:
            lower *= 2 if earlier < bit else 1
        shape = held.shape
        parts = [v.reshape((-1, 1, lower) + shape[1:]) for v in (first, second)]
        held = jnp.concatenate(parts, 1).reshape((shape[0] * 2,) + shape[1:])
        done.append(bit)
    return held.reshape((-1,) + shard.shape[1:])


def pick(value, which, lower):
    shape = value.shape
    split = value.reshape((-1, 2, lower) + shape[1:])
    return lax.dynamic_index_in_dim(split, which, 1, False).reshape((-1,) + shape[1:])


def scatter_rows(keep, send, total, me, order, sent_as):
    left = sorted(order)
    for at, bit in enumerate(order):
        if at > 0:
            lower = 1
            for other in left:
                lower *= 2 if other < bit else 1
            side = mine_of(me, bit)
            send = pick(keep, 1 - side, lower)
            keep = pick(keep, side, lower)
        got = swap(send, total, bit)
        keep = keep.astype(f32) + got.astype(f32)
        if at + 1 < len(order):
            keep = keep.astype(sent_as)
        left.remove(bit)
    return keep[0]


def core_columns(value, total, which):
    width = value.shape[1]
    split = value.reshape(value.shape[0], total // 2, 2, width // total)
    return lax.dynamic_index_in_dim(split, which, 2, False).reshape(value.shape[0], width // 2)


def sigma(v):
    return jax.nn.sigmoid(v)


def local(
    hidden_in,
    segments,
    cotangent,
    pre_gain,
    proj_weight,
    step_weight,
    conv_weight,
    conv_bias,
    gate_gain,
    out_weight,
    decay_log,
    step_bias,
    skip_gain,
):
    total = lax.axis_size("dp")
    me = lax.axis_index("dp")
    bits = total.bit_length() - 1
    order_a, order_b = orders(bits)
    core = mine_of(me, 0)
    rows, length, width = hidden_in.shape
    tokens = rows * length
    heads = decay_log.shape[0]
    depth = proj_weight.shape[0]
    conv_own, taps = conv_weight.shape
    gate_own = gate_gain.shape[0]
    inner = gate_own * total
    channels = inner // heads
    conv_all = conv_own * total
    state = (conv_all - inner) // 2
    small_own = conv_own * taps + conv_own + gate_own
    small_cols = -(-small_own // depth)
    tail = -(-(heads + 1 + small_cols) // 128) * 128

    smalls = jnp.concatenate([conv_weight.reshape(-1), conv_bias, gate_gain])
    smalls = jnp.pad(smalls, (0, depth * small_cols - small_own)).reshape(depth, small_cols)
    packed = jnp.concatenate([proj_weight[:, inner:], step_weight, pre_gain[:, None], smalls], 1)
    packed = jnp.pad(packed, ((0, 0), (0, conv_all + tail - packed.shape[1])))
    stream_w = gather_rows(packed, total, me, order_a)
    gate_w = gather_rows(proj_weight[:, :inner], total, me, order_b)
    half = width // 2
    out_w = [
        gather_rows(out_weight[:, :half], total, me, order_a),
        gather_rows(out_weight[:, half:], total, me, order_b),
    ]
    extra = stream_w[:, conv_all + heads : conv_all + heads + 1 + small_cols]
    gain_full = extra[:, 0].astype(f32)
    small_full = extra[:, 1:].reshape(total, depth * small_cols)
    kernel_full = small_full[:, : conv_own * taps].reshape(conv_all, taps).astype(f32)
    at = conv_own * taps
    bias_full = small_full[:, at : at + conv_own].reshape(conv_all).astype(f32)
    at = at + conv_own
    gate_full = small_full[:, at : at + gate_own].reshape(inner).astype(f32)

    u = hidden_in.reshape(tokens, width).astype(f32)
    upstream = cotangent.reshape(tokens, width)
    r = lax.rsqrt(jnp.mean(u * u, -1, keepdims=True) + 1e-05)
    normed = (u * r * gain_full).astype(bf16)
    wide = jnp.dot(normed, stream_w, preferred_element_type=f32)
    gate_part = jnp.dot(normed, gate_w, preferred_element_type=f32)
    stream = wide[:, :conv_all].reshape(rows, length, conv_all)
    step_raw = wide[:, conv_all : conv_all + heads].reshape(rows, length, heads)

    def back(v, offset):
        return v if offset == 0 else jnp.pad(v[:, :-offset], ((0, 0), (offset, 0), (0, 0)))

    def ahead(v, offset):
        return v if offset == 0 else jnp.pad(v[:, offset:], ((0, 0), (0, offset), (0, 0)))

    same = []
    for offset in range(taps):
        earlier = jnp.pad(segments[:, : length - offset], ((0, 0), (offset, 0)), constant_values=-1)
        same.append((earlier == segments).astype(f32)[:, :, None])
    convolved = bias_full
    for offset in range(taps):
        convolved = convolved + same[offset] * back(stream, offset) * kernel_full[:, taps - 1 - offset]
    conv_gate = sigma(convolved)
    activated = convolved * conv_gate
    values = activated[:, :, :inner].reshape(rows, length, heads, channels)
    input_map = activated[:, :, inner : inner + state]
    output_map = activated[:, :, inner + state :]
    pre = step_raw + step_bias
    step_size = jax.nn.softplus(pre)
    rate = jnp.exp(decay_log)
    log_decay = -rate * step_size
    causal = jnp.arange(length)[:, None] >= jnp.arange(length)[None, :]
    lower_ones = causal.astype(f32)
    inside = (segments[:, :, None] == segments[:, None, :]) & causal[None]
    inside = inside[:, None]
    cumulative = jnp.einsum("tu,buh->bht", lower_ones, log_decay, precision=lax.Precision.HIGHEST)
    gap = cumulative[:, :, :, None] - cumulative[:, :, None, :]
    decay = jnp.where(inside, jnp.exp(jnp.where(inside, gap, 0.0)), 0.0)
    scores = jnp.einsum("btn,bun->btu", output_map, input_map, precision=near)
    mixing = decay * scores[:, None]
    scaled = (values * step_size[..., None]).transpose(0, 2, 1, 3)
    mixed = jnp.einsum("bhtu,bhup->bhtp", mixing, scaled, precision=near)
    skip_each = jnp.repeat(skip_gain, channels)
    flat_values = activated[:, :, :inner].reshape(tokens, inner)
    y = mixed.transpose(0, 2, 1, 3).reshape(tokens, inner) + skip_each * flat_values
    gate_sig = sigma(gate_part)
    gate_silu = gate_part * gate_sig
    gated = y * gate_silu
    q = lax.rsqrt(jnp.mean(gated * gated, -1, keepdims=True) + 1e-05)
    gated_norm = (gated * q * gate_full).astype(bf16)

    branch = jnp.concatenate([jnp.dot(gated_norm, w, preferred_element_type=f32) for w in out_w], 1)
    output = (u + branch).astype(bf16)

    def both_halves(left, right):
        other = contract_first(core_columns(left, total, 1 - core), right).astype(bf16)
        own = contract_first(core_columns(left, total, core), right).astype(bf16)
        shape = (total // 2, left.shape[1] // total, right.shape[1])
        return own.reshape(shape), other.reshape(shape)

    def summed(left, right, order):
        own, other = both_halves(left, right)
        return scatter_rows(own, other, total, me, order, bf16)

    grad_out = [
        summed(gated_norm, upstream[:, :half], order_a),
        summed(gated_norm, upstream[:, half:], order_b),
    ]

    d_norm = contract_last(upstream[:, :half], out_w[0]) + contract_last(upstream[:, half:], out_w[1])
    grad_gate_gain = jnp.sum(d_norm * gated * q, 0)
    weighted = gate_full * d_norm
    d_gated = q * weighted - gated * (q * q * q) * jnp.mean(gated * weighted, -1, keepdims=True)
    d_y = d_gated * gate_silu
    d_gate = (d_gated * y * gate_sig * (1.0 + gate_part * (1.0 - gate_sig))).astype(bf16)
    quarter = inner // 2
    grad_gate = [
        summed(normed, d_gate[:, :quarter], order_a),
        summed(normed, d_gate[:, quarter:], order_b),
    ]

    grad_skip = jnp.sum((flat_values * d_y).reshape(tokens, heads, channels), (0, 2))
    d_y4 = d_y.reshape(rows, length, heads, channels).transpose(0, 2, 1, 3)
    d_mixing = jnp.einsum("bhtp,bhup->bhtu", d_y4, scaled, precision=near)
    d_scaled = jnp.einsum("bhtu,bhtp->bhup", mixing, d_y4, precision=near)
    d_scores = jnp.sum(d_mixing * decay, 1)
    spread = d_mixing * mixing
    d_cumulative = jnp.sum(spread, 3) - jnp.sum(spread, 2)
    d_output_map = jnp.einsum("btu,bun->btn", d_scores, input_map, precision=near)
    d_input_map = jnp.einsum("btu,btn->bun", d_scores, output_map, precision=near)
    d_log_decay = jnp.einsum(
        "tu,bht->buh", lower_ones, d_cumulative, precision=lax.Precision.HIGHEST
    )
    d_scaled = d_scaled.transpose(0, 2, 1, 3)
    d_step_size = jnp.sum(d_scaled * values, -1)
    d_values = (d_scaled * step_size[..., None]).reshape(rows, length, inner)
    d_values = d_values + (skip_each * d_y).reshape(rows, length, inner)
    grad_decay = jnp.sum(d_log_decay * log_decay, (0, 1))
    d_pre = (d_step_size - rate * d_log_decay) * sigma(pre)
    grad_bias = jnp.sum(d_pre, (0, 1))
    head_sums = jnp.stack([grad_decay, grad_bias, grad_skip])
    for bit in range(bits):
        head_sums = head_sums + swap(head_sums, total, bit)

    d_activated = jnp.concatenate([d_values, d_input_map, d_output_map], -1)
    d_convolved = d_activated * conv_gate * (1.0 + convolved * (1.0 - conv_gate))
    grad_conv_bias = jnp.sum(d_convolved, (0, 1))
    grad_taps = [None] * taps
    d_stream = 0.0
    for offset in range(taps):
        masked = same[offset] * d_convolved
        grad_taps[taps - 1 - offset] = jnp.sum(masked * back(stream, offset), (0, 1))
        d_stream = d_stream + ahead(masked, offset) * kernel_full[:, taps - 1 - offset]
    d_stream = d_stream.reshape(tokens, conv_all).astype(bf16)
    d_step = d_pre.reshape(tokens, heads).astype(bf16)
    middle = conv_all // 2
    grad_stream = [
        summed(normed, d_stream[:, :middle], order_a),
        summed(normed, d_stream[:, middle:], order_b),
    ]
    d_wide = jnp.pad(jnp.concatenate([d_stream, d_step], 1), ((0, 0), (0, tail - heads)))
    d_normed = contract_last(d_wide, stream_w) + contract_last(d_gate, gate_w)
    grad_pre = jnp.sum(d_normed * u * r, 0)
    lifted = gain_full * d_normed
    d_rows = r * lifted - u * (r * r * r) * jnp.mean(lifted * u, -1, keepdims=True)
    input_grad = upstream.astype(f32) + d_rows

    grad_kernel = jnp.stack(grad_taps, 1).reshape(total, conv_own * taps)
    small_grads = jnp.concatenate(
        [grad_kernel, grad_conv_bias.reshape(total, conv_own), grad_gate_gain.reshape(total, gate_own)],
        1,
    )
    small_grads = jnp.pad(small_grads, ((0, 0), (0, depth * small_cols - small_own)))
    tail_grads = jnp.concatenate(
        [
            contract_first(normed, d_step).reshape(total, depth, heads),
            grad_pre.reshape(total, depth, 1),
            small_grads.reshape(total, depth, small_cols),
        ],
        2,
    )
    tail_grads = jnp.pad(tail_grads, ((0, 0), (0, 0), (0, tail - tail_grads.shape[2])))
    tail_sum = scatter_rows(
        pick(tail_grads, core, 1), pick(tail_grads, 1 - core, 1), total, me, order_a, f32
    )
    small_sum = tail_sum[:, heads + 1 : heads + 1 + small_cols].reshape(-1)
    at = conv_own * taps
    return (
        output.reshape(rows, length, width),
        input_grad.reshape(rows, length, width),
        tail_sum[:, heads],
        jnp.concatenate(grad_gate + grad_stream, 1),
        tail_sum[:, :heads],
        small_sum[:at].reshape(conv_own, taps),
        small_sum[at : at + conv_own],
        small_sum[at + conv_own : at + conv_own + gate_own],
        jnp.concatenate(grad_out, 1),
        head_sums[0],
        head_sums[1],
        head_sums[2],
    )


def solution(mesh):
    split = P("dp", None)
    cube = P("dp", None, None)
    line = P("dp")
    return jax.shard_map(
        local,
        mesh=mesh,
        in_specs=(cube, split, cube, line, split, split, split, line, line, split, P(), P(), P()),
        out_specs=(cube, cube, line, split, split, split, line, line, split, P(), P(), P()),
        check_vma=False,
    )
```

```python
from functools import partial

import jax
import jax.numpy as jnp
from jax import lax
from jax.experimental import pallas as pl
from jax.experimental.pallas import tpu as pltpu
from jax.sharding import PartitionSpec as P

f32 = jnp.float32
bf16 = jnp.bfloat16
near = lax.Precision.HIGH


def sum_kernel(in_a, out_a, in_b, out_b, *rest):
    state = in_a.shape[1]
    rest[-1][:, :state] = in_a[...] + in_b[...]
    rest[-1][:, state:] = out_a[...] + out_b[...]


def sum_maps(one, other, after):
    rows, length, state = one[0].shape
    specs = [row_block(length, state)] * 4 + [pl.BlockSpec(a.shape, lambda i: (0, 0)) for a in after]
    return pl.pallas_call(
        sum_kernel,
        grid=(rows,),
        in_specs=specs,
        out_specs=row_block(length, 2 * state),
        out_shape=jax.ShapeDtypeStruct((rows, length, 2 * state), f32),
    )(*one, *other, *after)


def contract_last(left, right):
    return lax.dot_general(left, right, (((1,), (1,)), ((), ())), preferred_element_type=f32)


def contract_first(left, right):
    return lax.dot_general(left, right, (((0,), (0,)), ((), ())), preferred_element_type=f32)


def orders(bits):
    rest = list(range(1, bits))
    return rest[2:], [0] + rest[:2], [0] + rest[:2][::-1]


def swap(value, total, bit):
    return lax.ppermute(value, "dp", [(i, i ^ (1 << bit)) for i in range(total)])


def mine_of(me, bit):
    return lax.rem(lax.div(me, 1 << bit), 2)


def gather_rows(held, total, me, order, done):
    done = list(done)
    for bit in reversed(order):
        got = swap(held, total, bit)
        side = mine_of(me, bit) == 0
        first, second = jnp.where(side, held, got), jnp.where(side, got, held)
        lower = 1
        for earlier in done:
            lower *= 2 if earlier < bit else 1
        shape = held.shape
        parts = [v.reshape((-1, 1, lower) + shape[1:]) for v in (first, second)]
        held = jnp.concatenate(parts, 1).reshape((shape[0] * 2,) + shape[1:])
        done.append(bit)
    return held


def pick(value, which, lower):
    shape = value.shape
    split = value.reshape((-1, 2, lower) + shape[1:])
    return lax.dynamic_index_in_dim(split, which, 1, False).reshape((-1,) + shape[1:])


def scatter_rows(keep, total, me, order, left):
    left = sorted(left)
    received = []
    for bit in order:
        lower = 1
        for other in left:
            lower *= 2 if other < bit else 1
        side = mine_of(me, bit)
        sent_as = keep.dtype
        got = swap(pick(keep, 1 - side, lower), total, bit)
        received.append(got.reshape(-1, got.shape[-1])[:16, :128])
        keep = pick(keep, side, lower).astype(f32) + got.astype(f32)
        left.remove(bit)
        keep = keep.astype(sent_as) if left else keep
    return keep, received


def sigma(v):
    return jax.nn.sigmoid(v)


LAST = (((1,), (1,)), ((), ()))
PLAIN = (((1,), (0,)), ((), ()))


def close_dot(left, right, dims):
    left_high = left.astype(bf16)
    left_low = (left - left_high.astype(f32)).astype(bf16)
    right_high = right.astype(bf16)
    right_low = (right - right_high.astype(f32)).astype(bf16)

    def dot(a, b):
        return lax.dot_general(a, b, dims, preferred_element_type=f32)

    return dot(left_high, right_high) + (dot(left_high, right_low) + dot(left_low, right_high))


def lanes_of(length, lanes, channels):
    return lax.broadcasted_iota(jnp.int32, (length, lanes), 1) // channels


def forward_kernel(
    channels, values_ref, in_ref, out_ref, ccol_ref, crow_ref, step_ref, segc_ref, segr_ref, skip_ref, y_ref
):
    length, inner = values_ref.shape
    per = 128 // channels
    which = lanes_of(length, 128, channels)
    t = lax.broadcasted_iota(jnp.int32, (length, length), 0)
    s = lax.broadcasted_iota(jnp.int32, (length, length), 1)
    mask = (segc_ref[...] == segr_ref[...]) & (t >= s)
    scores = jnp.where(mask, close_dot(out_ref[...], in_ref[...], LAST), 0.0)
    for block in range(inner // 128):
        cols = slice(block * 128, (block + 1) * 128)
        values = values_ref[:, cols]
        mixes, parts = [], []
        for k in range(per):
            h = block * per + k
            gap = ccol_ref[:, h : h + 1] - crow_ref[h : h + 1, :]
            mixes.append(jnp.exp(jnp.where(mask, gap, 0.0)) * scores)
            parts.append(jnp.where(which == k, values * step_ref[:, h : h + 1], 0.0))
        mixed = close_dot(jnp.concatenate(mixes, 1), jnp.concatenate(parts, 0), PLAIN)
        y_ref[:, cols] = mixed + skip_ref[:, cols] * values


def backward_kernel(
    channels,
    first,
    values_ref,
    in_ref,
    out_ref,
    ccol_ref,
    crow_ref,
    step_ref,
    segc_ref,
    segr_ref,
    skip_ref,
    dy_ref,
    *rest,
):
    dvalues_ref, din_ref, dout_ref, dstep_ref, drow_ref, dcol_ref = rest[-6:]
    length, inner = values_ref.shape
    heads = inner // channels
    per = 128 // channels
    which = lanes_of(length, 128, channels)
    head_lane = lax.broadcasted_iota(jnp.int32, (length, heads), 1)
    s = lax.broadcasted_iota(jnp.int32, (length, length), 0)
    t = lax.broadcasted_iota(jnp.int32, (length, length), 1)
    mask = (segc_ref[...] == segr_ref[...]) & (t >= s)
    scores = jnp.where(mask, close_dot(in_ref[...], out_ref[...], LAST), 0.0)
    d_scores = jnp.zeros((length, length), f32)
    d_step = jnp.zeros((length, heads), f32)
    d_col = jnp.zeros((length, heads), f32)
    for block in range(inner // 128):
        cols = slice(block * 128, (block + 1) * 128)
        values = values_ref[:, cols]
        dy = dy_ref[:, cols]
        decays, mixes, parts = [], [], []
        step = jnp.zeros((length, 128), f32)
        for k in range(per):
            h = first + block * per + k
            gap = crow_ref[h : h + 1, :] - ccol_ref[:, h : h + 1]
            decays.append(jnp.exp(jnp.where(mask, gap, 0.0)))
            mixes.append(decays[k] * scores)
            parts.append(jnp.where(which == k, dy, 0.0))
            step = jnp.where(which == k, step_ref[:, h : h + 1], step)
        each = jnp.concatenate(parts, 0)
        d_mix = close_dot(values * step, each, LAST)
        d_scaled = close_dot(jnp.concatenate(mixes, 1), each, PLAIN)
        dvalues_ref[:, cols] = d_scaled * step + skip_ref[:, cols] * dy
        product = d_scaled * values
        for k in range(per):
            h = block * per + k
            d_own = d_mix[:, k * length : (k + 1) * length]
            d_scores = d_scores + d_own * decays[k]
            spread = d_own * mixes[k]
            drow_ref[h : h + 1, :] = jnp.sum(spread, 0, keepdims=True)
            d_col = jnp.where(head_lane == h, jnp.sum(spread, 1, keepdims=True), d_col)
            own = jnp.sum(jnp.where(which == k, product, 0.0), 1, keepdims=True)
            d_step = jnp.where(head_lane == h, own, d_step)
    dstep_ref[...] = d_step
    dcol_ref[...] = d_col
    d_scores = jnp.where(mask, d_scores, 0.0)
    din_ref[...] = close_dot(d_scores, out_ref[...], PLAIN)
    dout_ref[...] = close_dot(d_scores.T, in_ref[...], PLAIN)


def row_block(height, width, column=0):
    return pl.BlockSpec((None, height, width), lambda i: (i, 0, column))


def mixer_call(activated, ccol, crow, step_size, segments, skip_each, state, part, parts, d_y=None, after=()):
    rows, length, conv_all = activated.shape
    heads = step_size.shape[2]
    inner = conv_all - 2 * state
    wide = inner // parts
    some = heads // parts
    specs = [
        row_block(length, wide, part),
        row_block(length, state, inner // state),
        row_block(length, state, inner // state + 1),
        row_block(length, heads),
        row_block(heads, length),
        row_block(length, heads),
        row_block(length, 1),
        row_block(1, length),
        pl.BlockSpec((1, wide), lambda i: (0, part)),
    ]
    operands = [activated, activated, activated, ccol, crow, step_size]
    operands += [segments[:, :, None], segments[:, None, :], skip_each[None]]
    params = pltpu.CompilerParams(vmem_limit_bytes=40 * 2**20)
    cost = pl.CostEstimate(flops=6 * 10**9, bytes_accessed=16 * 2**20, transcendentals=2**20)
    if d_y is None:
        return pl.pallas_call(
            partial(forward_kernel, inner // heads),
            grid=(rows,),
            in_specs=specs,
            out_specs=row_block(length, wide),
            out_shape=jax.ShapeDtypeStruct((rows, length, wide), f32),
            compiler_params=params,
            cost_estimate=cost,
        )(*operands)
    specs.append(row_block(length, wide, part))
    specs += [pl.BlockSpec(a.shape, lambda i: (0, 0)) for a in after]
    shapes = [(length, wide), (length, state), (length, state), (length, some), (some, length), (length, some)]
    return pl.pallas_call(
        partial(backward_kernel, inner // heads, part * some),
        grid=(rows,),
        in_specs=specs,
        out_specs=[row_block(*shape) for shape in shapes],
        out_shape=[jax.ShapeDtypeStruct((rows,) + shape, f32) for shape in shapes],
        compiler_params=params,
        cost_estimate=cost,
    )(*operands, d_y, *after)


def local(
    hidden_in,
    segments,
    cotangent,
    pre_gain,
    proj_weight,
    step_weight,
    conv_weight,
    conv_bias,
    gate_gain,
    out_weight,
    decay_log,
    step_bias,
    skip_gain,
):
    total = lax.axis_size("dp")
    me = lax.axis_index("dp")
    bits = total.bit_length() - 1
    far, order_a, order_b = orders(bits)
    everything = list(range(bits))
    rows, length, width = hidden_in.shape
    tokens = rows * length
    heads = decay_log.shape[0]
    depth = proj_weight.shape[0]
    conv_own, taps = conv_weight.shape
    gate_own = gate_gain.shape[0]
    inner = gate_own * total
    channels = inner // heads
    conv_all = conv_own * total
    state = (conv_all - inner) // 2
    small_own = conv_own * taps + conv_own + gate_own
    small_cols = -(-small_own // depth)
    tail = -(-(heads + 1 + small_cols) // 128) * 128

    smalls = jnp.concatenate([conv_weight.reshape(-1), conv_bias, gate_gain])
    smalls = jnp.pad(smalls, (0, depth * small_cols - small_own)).reshape(depth, small_cols)
    packed = jnp.concatenate([proj_weight[:, inner:], step_weight, pre_gain[:, None], smalls], 1)
    packed = jnp.pad(packed, ((0, 0), (0, conv_all + tail - packed.shape[1])))
    half = width // 2

    def gathered(shard, order):
        return gather_rows(shard[None], total, me, order + far, []).reshape(-1, shard.shape[1])

    stream_w = gathered(packed, order_a)
    gate_w = gathered(proj_weight[:, :inner], order_b)
    out_w = [gathered(out_weight[:, :half], order_a), gathered(out_weight[:, half:], order_b)]
    extra = stream_w[:, conv_all + heads : conv_all + heads + 1 + small_cols]
    gain_full = extra[:, 0].astype(f32)
    small_full = extra[:, 1:].reshape(total, depth * small_cols)
    kernel_full = small_full[:, : conv_own * taps].reshape(conv_all, taps).astype(f32)
    at = conv_own * taps
    bias_full = small_full[:, at : at + conv_own].reshape(conv_all).astype(f32)
    at = at + conv_own
    gate_full = small_full[:, at : at + gate_own].reshape(inner).astype(f32)

    u = hidden_in.reshape(tokens, width).astype(f32)
    upstream = cotangent.reshape(tokens, width)
    r = lax.rsqrt(jnp.mean(u * u, -1, keepdims=True) + 1e-05)
    normed = (u * r * gain_full).astype(bf16)
    wide = jnp.dot(normed, stream_w, preferred_element_type=f32)
    gate_part = jnp.dot(normed, gate_w, preferred_element_type=f32)
    stream = wide[:, :conv_all].reshape(rows, length, conv_all)
    step_raw = wide[:, conv_all : conv_all + heads].reshape(rows, length, heads)

    def behind(v, offset):
        return v if offset == 0 else jnp.pad(v[:, :-offset], ((0, 0), (offset, 0), (0, 0)))

    def ahead(v, offset):
        return v if offset == 0 else jnp.pad(v[:, offset:], ((0, 0), (0, offset), (0, 0)))

    same = []
    for offset in range(taps):
        earlier = jnp.pad(segments[:, : length - offset], ((0, 0), (offset, 0)), constant_values=-1)
        same.append((earlier == segments).astype(f32)[:, :, None])
    convolved = bias_full
    for offset in range(taps):
        convolved = convolved + same[offset] * behind(stream, offset) * kernel_full[:, taps - 1 - offset]
    conv_gate = sigma(convolved)
    activated = convolved * conv_gate
    pre = step_raw + step_bias
    step_size = jax.nn.softplus(pre)
    rate = jnp.exp(decay_log)
    log_decay = -rate * step_size
    causal = jnp.arange(length)[:, None] >= jnp.arange(length)[None, :]
    lower_ones = causal.astype(f32)
    ccol = jnp.einsum("tu,buh->bth", lower_ones, log_decay, precision=lax.Precision.HIGHEST)
    crow = ccol.transpose(0, 2, 1)
    skip_each = jnp.repeat(skip_gain, channels)
    mixer = partial(mixer_call, activated, ccol, crow, step_size, segments, skip_each, state)
    flat_values = activated[:, :, :inner].reshape(tokens, inner)
    y = mixer(0, 1).reshape(tokens, inner)
    gate_sig = sigma(gate_part)
    gate_silu = gate_part * gate_sig
    gated = y * gate_silu
    q = lax.rsqrt(jnp.mean(gated * gated, -1, keepdims=True) + 1e-05)
    gated_norm = (gated * q * gate_full).astype(bf16)

    branch = jnp.concatenate([jnp.dot(gated_norm, w, preferred_element_type=f32) for w in out_w], 1)
    output = (u + branch).astype(bf16)

    def summed(left, right, order):
        terms = contract_first(left, right).astype(bf16)
        terms = terms.reshape(total, left.shape[1] // total, right.shape[1])
        return scatter_rows(terms, total, me, order, everything)

    def finished(*chains):
        flat = [chain[0].reshape(chain[0].shape[0], depth, -1) for chain in chains]
        return scatter_rows(jnp.concatenate(flat, 2), total, me, far, far)[0].reshape(depth, -1)

    out_sums = summed(gated_norm, upstream, order_a)

    d_norm = contract_last(upstream[:, :half], out_w[0]) + contract_last(upstream[:, half:], out_w[1])
    grad_gate_gain = jnp.sum(d_norm * gated * q, 0)
    weighted = gate_full * d_norm
    d_gated = q * weighted - gated * (q * q * q) * jnp.mean(gated * weighted, -1, keepdims=True)
    d_y = d_gated * gate_silu
    d_gate = (d_gated * y * gate_sig * (1.0 + gate_part * (1.0 - gate_sig))).astype(bf16)
    gate_sums = summed(normed, d_gate, order_b)

    grad_skip = jnp.sum(jnp.sum(flat_values * d_y, 0).reshape(heads, channels), 1)
    d_y3 = d_y.reshape(rows, length, inner)

    def waits(*pairs):
        return tuple(sums[1][stage] for sums, stage in pairs)

    order_of_waits = (waits((out_sums, 0)), waits((out_sums, 1), (gate_sums, 0)))
    backs = [mixer(part, 2, d_y3, after) for part, after in enumerate(order_of_waits)]
    d_maps = sum_maps(backs[0][1:3], backs[1][1:3], waits((out_sums, 2), (gate_sums, 1)))
    d_step_size = jnp.concatenate([back[3] for back in backs], 2)
    d_cumulative = jnp.concatenate([back[4] for back in backs], 1)
    d_cumulative = d_cumulative - jnp.concatenate([back[5] for back in backs], 2).transpose(0, 2, 1)
    d_log_decay = jnp.einsum(
        "tu,bht->buh", lower_ones, d_cumulative, precision=lax.Precision.HIGHEST
    )
    grad_decay = jnp.sum(d_log_decay * log_decay, (0, 1))
    d_pre = (d_step_size - rate * d_log_decay) * sigma(pre)
    grad_bias = jnp.sum(d_pre, (0, 1))
    head_sums = jnp.stack([grad_decay, grad_bias, grad_skip])
    head_cols = -(-head_sums.size // depth)
    head_sums = jnp.pad(head_sums.reshape(-1), (0, depth * head_cols - head_sums.size))
    head_sums = jnp.broadcast_to(head_sums.reshape(1, depth, head_cols), (total, depth, head_cols))

    def conv_back(d_activated, start, stop):
        own = convolved[:, :, start:stop]
        gate = sigma(own)
        d_convolved = d_activated * gate * (1.0 + own * (1.0 - gate))
        source = stream[:, :, start:stop]
        grads = [None] * taps
        d_source = 0.0
        for offset in range(taps):
            masked = same[offset] * d_convolved
            grads[taps - 1 - offset] = jnp.sum(masked * behind(source, offset), (0, 1))
            d_source = d_source + ahead(masked, offset) * kernel_full[start:stop, taps - 1 - offset]
        d_source = d_source.reshape(tokens, stop - start).astype(bf16)
        return d_source, jnp.stack(grads, 1), jnp.sum(d_convolved, (0, 1))

    middle = inner // 2
    pieces = [
        conv_back(backs[0][0], 0, middle),
        conv_back(backs[1][0], middle, inner),
        conv_back(d_maps, inner, conv_all),
    ]
    grad_taps = jnp.concatenate([piece[1] for piece in pieces], 0)
    grad_conv_bias = jnp.concatenate([piece[2] for piece in pieces], 0)
    d_stream = jnp.concatenate([piece[0] for piece in pieces], 1)
    d_step = d_pre.reshape(tokens, heads).astype(bf16)
    stream_sums = [
        summed(normed, piece[0], order) for piece, order in zip(pieces, (order_a, order_b))
    ]
    d_wide = jnp.pad(jnp.concatenate([d_stream, d_step], 1), ((0, 0), (0, tail - heads)))
    d_normed = contract_last(d_wide, stream_w) + contract_last(d_gate, gate_w)
    grad_pre = jnp.sum(d_normed * u * r, 0)
    lifted = gain_full * d_normed
    d_rows = r * lifted - u * (r * r * r) * jnp.mean(lifted * u, -1, keepdims=True)
    input_grad = upstream.astype(f32) + d_rows

    grad_kernel = grad_taps.reshape(total, conv_own * taps)
    small_grads = jnp.concatenate(
        [grad_kernel, grad_conv_bias.reshape(total, conv_own), grad_gate_gain.reshape(total, gate_own)],
        1,
    )
    small_grads = jnp.pad(small_grads, ((0, 0), (0, depth * small_cols - small_own)))
    maps = 2 * state
    last = contract_first(normed, d_wide[:, inner : conv_all + heads])
    tail_grads = jnp.concatenate(
        [
            last.reshape(total, depth, maps + heads),
            grad_pre.reshape(total, depth, 1),
            small_grads.reshape(total, depth, small_cols),
            head_sums,
        ],
        2,
    )
    over = -tail_grads.shape[2] % 128
    tail_grads = jnp.pad(tail_grads, ((0, 0), (0, 0), (0, over)))
    tail_sum = scatter_rows(tail_grads, total, me, order_a + far, everything)[0][0]
    early = finished(out_sums, gate_sums)
    late = finished(*stream_sums)
    grad_proj = jnp.concatenate([early[:, -inner:], late, tail_sum[:, :maps]], 1)
    grad_out = early[:, :-inner].reshape(gate_own, width)
    tail_sum = tail_sum[:, maps:]
    head_at = heads + 1 + small_cols
    head_sums = tail_sum[:, head_at : head_at + head_cols].reshape(-1)[: 3 * heads]
    head_sums = head_sums.reshape(3, heads)
    small_sum = tail_sum[:, heads + 1 : heads + 1 + small_cols].reshape(-1)
    at = conv_own * taps
    return (
        output.reshape(rows, length, width),
        input_grad.reshape(rows, length, width),
        tail_sum[:, heads],
        grad_proj,
        tail_sum[:, :heads],
        small_sum[:at].reshape(conv_own, taps),
        small_sum[at : at + conv_own],
        small_sum[at + conv_own : at + conv_own + gate_own],
        grad_out,
        head_sums[0],
        head_sums[1],
        head_sums[2],
    )


def solution(mesh):
    split = P("dp", None)
    cube = P("dp", None, None)
    line = P("dp")
    return jax.shard_map(
        local,
        mesh=mesh,
        in_specs=(cube, split, cube, line, split, split, split, line, line, split, P(), P(), P()),
        out_specs=(cube, cube, line, split, split, split, line, line, split, P(), P(), P()),
        check_vma=False,
    )
```
